256 devices in a mesh: seq: 16 (over y, x), tensor: 16 (over z, core).
Axes of the slice: x: 4, y: 4, z: 8, core: 2. Of those that a mesh axis runs over, the one named last changes fastest.
Arguments:
- hidden_in: bfloat16 [1024, 8192], P('seq'), may hold values from -24 to 24
- gate_codes: bfloat16 [8192, 53248], P('seq', 'tensor'), may hold values from -8 to 7, as said below
- up_codes: bfloat16 [8192, 53248], P('seq', 'tensor'), may hold values from -8 to 7, as said below
- gate_scale: float32 [53248], P('tensor'), may hold values from 0.0015 to 0.006
- up_scale: float32 [53248], P('tensor'), may hold values from 0.0015 to 0.006
- down_codes: bfloat16 [53248, 8192], P('tensor', 'seq'), may hold values from -8 to 7, as said below
- down_scale: float32 [8192], P('seq'), may hold values from 0.0007 to 0.0028
- sign_bits: int32 [53248], P('tensor'), may hold values from 0 to 1
- had52: int32 [52, 52], replicated, may hold values from -1 to 1, as said below
Outputs:
- mixed: bfloat16 [1024, 8192], P('tensor', 'seq')
The draws below stay inside these ranges and needn't reach their ends.
Inputs may be any that keep to these rules, and one draw needn't show every extreme that they name: `gate_codes`: every entry is a whole number. `up_codes`: every entry is a whole number. `down_codes`: every entry is a whole number. had52 is a Hadamard matrix: entries -1 or 1, rows mutually orthogonal.
All inputs are finite; a program needn't handle non-finite values.
Results may differ from the reference program's by a relative error of at most 0.024.
Values may be sent and summed in bfloat16 or wider, within the bound.
A program may use at most 192 MiB of HBM per device.

```python
import math
import jax
import jax.numpy as jnp
import numpy as np
from jax import lax

D = 8192
FACTOR = 52
SPAN = 1024
FF = 53248
TOKENS = 1024


def paley_base():
    elements = [(first_part, second_part) for first_part in range(5) for second_part in range(5)]

    def product_of(left_elem, right_elem):
        return ((left_elem[0] * right_elem[0] + 2 * left_elem[1] * right_elem[1]) % 5, (left_elem[0] * right_elem[1] + left_elem[1] * right_elem[0]) % 5)
    squares = set((product_of(member, member) for member in elements if member != (0, 0)))
    jacobsthal = np.zeros((25, 25))
    for row_index, left_elem in enumerate(elements):
        for col_index, right_elem in enumerate(elements):
            difference = ((left_elem[0] - right_elem[0]) % 5, (left_elem[1] - right_elem[1]) % 5)
            if difference == (0, 0):
                jacobsthal[row_index, col_index] = 0.0
            elif difference in squares:
                jacobsthal[row_index, col_index] = 1.0
            else:
                jacobsthal[row_index, col_index] = -1.0
    conference = np.zeros((26, 26))
    conference[0, 1:] = 1.0
    conference[1:, 0] = 1.0
    conference[1:, 1:] = jacobsthal
    upper_block = np.array([[1.0, 1.0], [1.0, -1.0]])
    lower_block = np.array([[1.0, -1.0], [-1.0, -1.0]])
    return np.kron(conference, upper_block) + np.kron(np.eye(26), lower_block)


def draw_codes(key, rows_count, cols_count):
    return jax.random.randint(key, (rows_count, cols_count), -8, 8).astype(jnp.float32).astype(jnp.bfloat16)


def draw_gate_codes(key, part):
    key = jax.random.fold_in(key, 3)
    return draw_codes(key, D, FF)


def draw_up_codes(key, part):
    key = jax.random.fold_in(key, 5)
    return draw_codes(key, D, FF)


def draw_down_codes(key, part):
    key = jax.random.fold_in(key, 7)
    return draw_codes(key, FF, D)


def draw_had52(key, part):
    key = jax.random.fold_in(key, 11)
    base = jnp.asarray(paley_base(), jnp.int32)
    row_key, col_key, rsign_key, csign_key = jax.random.split(key, 4)
    row_order = jax.random.permutation(row_key, FACTOR)
    col_order = jax.random.permutation(col_key, FACTOR)
    row_signs = 1 - 2 * jax.random.randint(rsign_key, (FACTOR,), 0, 2)
    col_signs = 1 - 2 * jax.random.randint(csign_key, (FACTOR,), 0, 2)
    shuffled = base[row_order][:, col_order]
    return (shuffled * row_signs[:, None] * col_signs[None, :]).astype(jnp.int32)


def place_ends(values, key, smallest, top_value):
    spot = [jax.random.randint(jax.random.fold_in(key, axis), (), 0, length) for axis, length in enumerate(values.shape)]
    main_axis = values.shape.index(max(values.shape))
    next_to = spot[:main_axis] + [(spot[main_axis] + 1) % values.shape[main_axis]] + spot[main_axis + 1:]
    return values.at[tuple(spot)].set(smallest).at[tuple(next_to)].set(top_value)


def levels(own_key, extent, cuts, smallest, high):
    def one(axis_at, shards_of):
        draws = jax.random.uniform(jax.random.fold_in(jax.random.fold_in(own_key, 6), axis_at), (shards_of,), jnp.float32, smallest / len(cuts), high / len(cuts))
        return jnp.repeat(jnp.exp(draws), extent[axis_at] // shards_of).reshape((-1,) + (1,) * (len(extent) - axis_at - 1))

    level = one(*cuts[0])
    for cut in cuts[1:]:
        level = level * one(*cut)
    return level


def bell_draw(own_key, extent, spread, limit, pieces=(), held_as=jnp.bfloat16):
    drawn = spread * jax.random.normal(own_key, extent, jnp.float32)
    if pieces:
        drawn = drawn * levels(own_key, extent, pieces, -0.22, 0.18)
    return jnp.clip(drawn, -limit, limit).astype(held_as)


def setup_inputs(seed: int = 0) -> dict:
    key_list = jax.random.split(jax.random.key(seed), 10)
    hidden_in = bell_draw(key_list[0], (TOKENS, D), 4.0, 24.0, ((0, 16),))
    gate_codes = draw_gate_codes(jax.random.fold_in(key_list[9], 71), 0)
    up_codes = draw_up_codes(jax.random.fold_in(key_list[9], 71), 0)
    gate_scale = jnp.clip(jnp.exp(math.log(0.006) - 1.3862944 * jax.random.uniform(key_list[3], (FF,), jnp.float32) ** levels(key_list[3], (FF,), ((0, 16),), -0.2, 0.2)), 0.0015, 0.006)
    up_scale = jnp.clip(jnp.exp(math.log(0.006) - 1.3862944 * jax.random.uniform(key_list[4], (FF,), jnp.float32) ** levels(key_list[4], (FF,), ((0, 16),), -0.2, 0.2)), 0.0015, 0.006)
    down_codes = draw_down_codes(jax.random.fold_in(key_list[9], 71), 0)
    down_scale = jnp.clip(jnp.exp(math.log(0.0028) - 1.3862944 * jax.random.uniform(key_list[6], (D,), jnp.float32) ** levels(key_list[6], (D,), ((0, 16),), -0.2, 0.2)), 0.0007, 0.0028)
    sign_bits = place_ends(jax.random.randint(key_list[7], (FF,), 0, 2), jax.random.fold_in(key_list[7], 1), 0, 1).astype(jnp.int32)
    had52 = draw_had52(jax.random.fold_in(key_list[9], 71), 0)
    return {"hidden_in": hidden_in, "gate_codes": gate_codes, "up_codes": up_codes, "gate_scale": gate_scale, "up_scale": up_scale, "down_codes": down_codes, "down_scale": down_scale, "sign_bits": sign_bits, "had52": had52}


def sylvester(length):
    indices = jnp.arange(length, dtype=jnp.int32)
    common_bits = jnp.bitwise_and(indices[:, None], indices[None, :])
    ones_count = jnp.zeros((length, length), jnp.int32)
    for shift_by in range(length.bit_length() - 1):
        ones_count = ones_count + jnp.bitwise_and(jnp.right_shift(common_bits, shift_by), 1)
    return (1 - 2 * (ones_count % 2)).astype(jnp.float32)

def reference(hidden_in, gate_codes, up_codes, gate_scale, up_scale, down_codes, down_scale, sign_bits, had52):
    values = hidden_in.astype(jnp.float32)
    normed = (values * lax.rsqrt(lax.optimization_barrier(jnp.mean(values * values, axis=1, keepdims=True)) + 1e-05)).astype(jnp.bfloat16)
    gate = jnp.dot(normed, gate_codes, preferred_element_type=jnp.float32) * gate_scale
    up = jnp.dot(normed, up_codes, preferred_element_type=jnp.float32) * up_scale
    activated = (jax.nn.silu(gate) * up).astype(jnp.bfloat16)
    flipped = activated.astype(jnp.float32) * (1 - 2 * sign_bits).astype(jnp.float32)
    shaped = flipped.reshape(TOKENS, SPAN, FACTOR)
    first = jnp.einsum('rba,ca->rbc', shaped, had52.astype(jnp.float32), precision=lax.Precision.HIGHEST)
    second = jnp.einsum('rba,cb->rca', first, sylvester(SPAN), precision=lax.Precision.HIGHEST)
    rotated = (second.reshape(TOKENS, FF) * (1.0 / math.sqrt(FF))).astype(jnp.bfloat16)
    return (jnp.dot(rotated, down_codes, preferred_element_type=jnp.float32) * down_scale).astype(jnp.bfloat16)
```

```python
import functools
import math

import jax
import jax.numpy as jnp
import ml_dtypes
import numpy as np
from jax import lax
from jax.experimental import pallas as pl
from jax.experimental.pallas import tpu as pltpu
from jax.sharding import PartitionSpec as P

FF = 53248
SIDE = 4
MESH = pl.DeviceIdType.MESH
F32 = jnp.float32
BF16 = jnp.bfloat16


def mod(value, by):
    return lax.rem(value, by)


def kernel(
    hid_hbm, gate_hbm, up_hbm, gate_scale, up_scale, down_hbm, down_scale, signs, had,
    pick, pick_t, spread, spread_t,
    out_ref,
    hid, x, w, wd, rot, ring, ring2, fin, inv, z1s, z1r, z2s, z2r, ag, outs, outr,
    load_sem, xs, xr, core_sem, r1s, r1r, r2s, r2r, z1ss, z1rs, z2ss, z2rs, ags, agr, os, orr,
):
    seq = lax.axis_index("seq")
    ten = lax.axis_index("tensor")
    n_seq = SIDE * SIDE
    tokens, features = hid.shape
    depth = features // n_seq
    half_rows = tokens // 2
    n_ten = z1r.shape[0]
    groups = n_ten // 2
    width = ring.shape[-1]
    core = mod(ten, 2)
    zed = lax.div(ten, 2)
    other = zed * 2 + 1 - core
    step_a = 1 + (SIDE - 1) * core
    step_b = SIDE - (SIDE - 1) * core
    pos_x, pos_y = mod(seq, SIDE), lax.div(seq, SIDE)
    pa = pos_x * (1 - core) + pos_y * core
    pb = pos_y * (1 - core) + pos_x * core

    def at(a, b):
        return mod(a + 2 * SIDE, SIDE) * step_a + mod(b + 2 * SIDE, SIDE) * step_b

    def remote(src, dst, send, recv, device):
        return pltpu.make_async_remote_copy(
            src_ref=src, dst_ref=dst, send_sem=send, recv_sem=recv, device_id=device, device_id_type=MESH
        )

    loads = [pltpu.make_async_copy(hid_hbm, hid, load_sem.at[0])]
    for j, (source, part) in enumerate(((gate_hbm, 0), (gate_hbm, 1), (up_hbm, 0), (up_hbm, 1))):
        loads.append(
            pltpu.make_async_copy(source.at[:, part * width : (part + 1) * width], w.at[j], load_sem.at[1 + j])
        )
    for h in range(2):
        loads.append(
            pltpu.make_async_copy(down_hbm.at[h * width : (h + 1) * width, :], wd.at[h], load_sem.at[5 + h])
        )
    for load in loads:
        load.start()

    barrier = pltpu.get_barrier_semaphore()

    def greet_seq(d, c):
        pl.semaphore_signal(barrier, inc=1, device_id={"seq": mod(seq + d, n_seq)}, device_id_type=MESH)
        return c

    def greet_ten(d, c):
        pl.semaphore_signal(barrier, inc=1, device_id={"tensor": mod(ten + d, n_ten)}, device_id_type=MESH)
        return c

    lax.fori_loop(1, n_seq, greet_seq, 0)
    lax.fori_loop(1, n_ten, greet_ten, 0)
    pl.semaphore_wait(barrier, n_seq + n_ten - 2)

    my_rows = pl.ds(pl.multiple_of(core * half_rows, half_rows), half_rows)

    def piece(d):
        peer = mod(seq + d, n_seq)
        return remote(
            hid_hbm.at[my_rows, pl.ds(pl.multiple_of(peer * depth, depth), depth)],
            x.at[core, seq],
            xs.at[d],
            xr.at[d],
            {"seq": peer},
        )

    def send_piece(d, c):
        piece(d).start()
        return c

    lax.fori_loop(1, n_seq, send_piece, 0)
    own = pltpu.make_async_copy(
        hid_hbm.at[my_rows, pl.ds(pl.multiple_of(seq * depth, depth), depth)], x.at[core, seq], xs.at[0]
    )
    own.start()

    rows_at_once = 128

    def build(r, c):
        rows = pl.ds(pl.multiple_of(r * rows_at_once, rows_at_once), rows_at_once)
        mixed = lax.dot_general(
            pick[rows, :], had[...].astype(F32).astype(BF16), (((1,), (1,)), ((), ())), preferred_element_type=F32
        )
        small = jnp.dot(mixed.astype(BF16), pick_t[...], preferred_element_type=F32)
        large = jnp.dot(spread[rows, :], spread_t[...], preferred_element_type=F32)
        rot[rows, :] = (small * large).astype(BF16)
        return c

    lax.fori_loop(0, width // rows_at_once, build, 0)
    loads[0].wait()
    chunk = min(1024, features)

    def squares(i, total):
        part = hid[:, pl.ds(pl.multiple_of(i * chunk, chunk), chunk)].astype(F32)
        return total + jnp.sum(part * part, axis=1, keepdims=True)

    total = lax.fori_loop(0, features // chunk, squares, jnp.zeros((tokens, 1), F32))
    inv[...] = jnp.broadcast_to(lax.rsqrt(total * (1.0 / features) + 1e-05), inv.shape)

    own.wait()

    def got_piece(d, c):
        piece(d).wait_recv()
        return c

    lax.fori_loop(1, n_seq, got_piece, 0)
    swap = remote(x.at[core], x.at[core], core_sem.at[0], core_sem.at[1], {"tensor": other})
    swap.start()
    for load in loads[1:5]:
        load.wait()
    swap.wait()

    def block_of(stream, step):
        return 3 - step if stream == 0 else 1 + step

    ahead = (1, SIDE - 1)

    def product(stream, step, j):
        a = pa + block_of(stream, step)
        rows = jnp.concatenate([x[stream, at(a, b)] for b in range(SIDE)], axis=0)
        return jnp.dot(rows, w[j], preferred_element_type=F32).reshape(SIDE, half_rows, width)

    def ring_copy(stream, step, j):
        return remote(
            ring.at[step, stream, j],
            ring.at[step + 1, stream, j],
            r1s.at[step, stream, j],
            r1r.at[step, stream, j],
            {"seq": at(pa + ahead[stream], pb)},
        )

    def ring2_copy(stream, step, j):
        if isinstance(step, int) and step == 0:
            source = ring.at[3, stream, j, mod(pb + block_of(stream, 0), SIDE)]
        else:
            source = ring2.at[step - 1, stream, j]
        return remote(
            source,
            ring2.at[step, stream, j],
            r2s.at[step, stream, j],
            r2r.at[step, stream, j],
            {"seq": at(pa, pb + ahead[stream])},
        )

    def first_step(j, c):
        for stream in range(2):
            ring[0, stream, j] = product(stream, 0, j).astype(BF16)
            ring_copy(stream, 0, j).start()
        return c

    lax.fori_loop(0, 4, first_step, 0)

    def next_step(i, c):
        step, j = 1 + lax.div(i, 4), mod(i, 4)
        for stream in range(2):
            value = product(stream, step, j)
            ring_copy(stream, step - 1, j).wait_recv()
            ring[step, stream, j] = (value + ring[step, stream, j].astype(F32)).astype(BF16)
            ring_copy(stream, step, j).start()
        return c

    lax.fori_loop(0, 8, next_step, 0)

    def last_steps(n, c):
        @pl.when(n < 4)
        def _():
            for stream in range(2):
                value = product(stream, 3, n)
                ring_copy(stream, 2, n).wait_recv()
                ring[3, stream, n] = (value + ring[3, stream, n].astype(F32)).astype(BF16)
                ring2_copy(stream, 0, n).start()

        for step in (1, 2, 3):

            @pl.when(jnp.logical_and(n >= step, n < 4 + step))
            def _():
                j = n - step
                for stream in range(2):
                    ring2_copy(stream, step - 1, j).wait_recv()
                    block = mod(pb + block_of(stream, step), SIDE)
                    value = ring[3, stream, j, block].astype(F32) + ring2[step - 1, stream, j].astype(F32)
                    if step < 3:
                        ring2[step - 1, stream, j] = value.astype(BF16)
                        ring2_copy(stream, step, j).start()
                    else:
                        fin[stream, j] = value

        return c

    lax.fori_loop(0, 7, last_steps, 0)

    for stream in range(2):
        rows = slice(stream * half_rows, (stream + 1) * half_rows)
        scale = inv[rows, 0:1]
        acts = []
        for h in range(2):
            cols = slice(h * width, (h + 1) * width)
            gate = fin[stream, h] * scale * gate_scale[:, cols]
            up = fin[stream, 2 + h] * scale * up_scale[:, cols]
            act = gate / (1.0 + jnp.exp(-gate)) * up
            acts.append(act * (1 - 2 * signs[:, cols]).astype(F32))
        in_group = tokens // groups
        per_stream = groups // 2
        for h, value in enumerate((acts[0] + acts[1], acts[0] - acts[1])):
            z1s[h, stream * per_stream : (stream + 1) * per_stream] = value.reshape(
                per_stream, in_group, width
            ).astype(BF16)

    def out_copy(d):
        peer = mod(ten + d, n_ten)
        return remote(
            z1s.at[mod(peer, 2), lax.div(peer, 2)], z1r.at[ten], z1ss.at[d], z1rs.at[d], {"tensor": peer}
        )

    def back_copy(d):
        peer = mod(ten + d, n_ten)
        return remote(z2s.at[peer], z2r.at[core, zed], z2ss.at[d], z2rs.at[d], {"tensor": peer})

    def start_of(copy):
        def go(d, c):
            copy(d).start()
            return c

        return go

    def arrival_of(copy):
        def go(d, c):
            copy(d).wait_recv()
            return c

        return go

    def departure_of(copy):
        def go(d, c):
            copy(d).wait_send()
            return c

        return go

    lax.fori_loop(1, n_ten, start_of(out_copy), 0)
    z1r[ten] = z1s[core, zed]
    lax.fori_loop(1, n_ten, arrival_of(out_copy), 0)
    spun = jnp.dot(
        z1r[...].astype(F32).reshape(n_ten * in_group, width).astype(BF16), rot[...], preferred_element_type=F32
    )
    spun = spun * (1.0 / math.sqrt(FF))
    span = 1
    while span < n_ten:
        pairs = spun.reshape(n_ten // (2 * span), 2, span * in_group, width)
        low, high = pairs[:, 0:1], pairs[:, 1:2]
        spun = jnp.concatenate([low + high, low - high], axis=1)
        span *= 2
    z2s[...] = spun.reshape(n_ten, in_group, width).astype(BF16)
    lax.fori_loop(1, n_ten, start_of(back_copy), 0)
    z2r[core, zed] = z2s[ten]
    lax.fori_loop(1, n_ten, arrival_of(back_copy), 0)
    for h in range(2):
        ag[seq, h] = z2r[h].astype(F32).reshape(tokens, width).astype(BF16)

    count = iter(range(30))
    pending = []

    def pass_on(s, h, target):
        n = next(count)
        copy = remote(ag.at[s, h], ag.at[s, h], ags.at[n], agr.at[s, h], {"seq": target})
        copy.start()
        pending.append(copy)

    def arrived(s, h):
        remote(ag.at[s, h], ag.at[s, h], ags.at[0], agr.at[s, h], {"seq": seq}).wait_recv()

    def send_first(s, a_step, b_step):
        for h0, h1 in ((0, 1), (1, 0)):
            pass_on(s, h0, at(pa + a_step, pb + b_step))
            pass_on(s, h1, at(pa - a_step, pb - b_step))

    def multiply(blocks):
        total = None
        for h in range(2):
            rows = jnp.concatenate([ag[s, h] for s in blocks], axis=0)
            part = jnp.dot(rows, wd[h], preferred_element_type=F32)
            total = part if total is None else total + part
        for i, s in enumerate(blocks):
            outs[s] = total[i * tokens : (i + 1) * tokens].astype(BF16)

            @pl.when(s != ten)
            def _():
                partial(s).start()

            @pl.when(s == ten)
            def _():
                outr[ten] = outs[s]

    def partial(s):
        return remote(outs.at[s], outr.at[ten], os.at[s], orr.at[ten], {"tensor": s})

    for load in loads[5:]:
        load.wait()
    send_first(seq, 1, 0)
    send_first(seq, 0, 1)
    arrived(at(pa, pb - 1), 0)
    pass_on(at(pa, pb - 1), 0, at(pa, pb + 1))
    arrived(at(pa, pb + 1), 1)
    pass_on(at(pa, pb + 1), 1, at(pa, pb - 1))
    arrived(at(pa, pb - 1), 1)
    send_first(at(pa, pb - 1), 1, 0)
    arrived(at(pa, pb + 1), 0)
    send_first(at(pa, pb + 1), 1, 0)

    def forward(b):
        arrived(at(pa - 1, b), 0)
        pass_on(at(pa - 1, b), 0, at(pa + 1, pb))
        arrived(at(pa + 1, b), 1)
        pass_on(at(pa + 1, b), 1, at(pa - 1, pb))

    def near(b):
        arrived(at(pa - 1, b), 1)
        arrived(at(pa + 1, b), 0)
        multiply([at(pa, b), at(pa - 1, b), at(pa + 1, b)])

    def far(b):
        arrived(at(pa + 2, b), 0)
        arrived(at(pa + 2, b), 1)
        multiply([at(pa + 2, b)])

    forward(pb)
    for h in range(2):
        arrived(at(pa, pb + 2), h)
    send_first(at(pa, pb + 2), 1, 0)
    near(pb)
    forward(pb - 1)
    far(pb)
    near(pb - 1)
    forward(pb + 1)
    far(pb - 1)
    near(pb + 1)
    forward(pb + 2)
    far(pb + 1)
    near(pb + 2)
    far(pb + 2)

    def from_tensor(t, c):
        @pl.when(t != ten)
        def _():
            remote(outs.at[t], outr.at[t], os.at[t], orr.at[t], {"tensor": t}).wait()

        return c

    lax.fori_loop(0, n_ten, from_tensor, 0)
    total = outr[0].astype(F32)
    for t in range(1, n_ten):
        total = total + outr[t].astype(F32)
    out_ref[...] = (total * down_scale[...]).astype(out_ref.dtype)

    def piece_left(d, c):
        piece(d).wait_send()
        return c

    lax.fori_loop(1, n_seq, piece_left, 0)

    def rings_left(j, c):
        for step in range(3):
            for stream in range(2):
                ring_copy(stream, step, j).wait_send()
                ring2_copy(stream, step, j).wait_send()
        return c

    lax.fori_loop(0, 4, rings_left, 0)
    lax.fori_loop(1, n_ten, departure_of(out_copy), 0)
    lax.fori_loop(1, n_ten, departure_of(back_copy), 0)
    for copy in pending:
        copy.wait_send()


def sylvester(length):
    matrix = np.ones((1, 1), np.float32)
    while matrix.shape[0] < length:
        matrix = np.kron(np.array([[1, 1], [1, -1]], np.float32), matrix)
    return matrix


def per_device(
    hidden_in, gate_codes, up_codes, gate_scale, up_scale, down_codes, down_scale, sign_bits, had52
):
    tokens, features = hidden_in.shape
    depth, block = gate_codes.shape
    width = block // 2
    factor = had52.shape[0]
    span = width // factor
    columns = down_codes.shape[1]
    n_seq = SIDE * SIDE
    n_ten = lax.axis_size("tensor")
    groups = n_ten // 2
    units = np.arange(width)
    pick = (units[:, None] % factor == np.arange(factor)[None, :]).astype(ml_dtypes.bfloat16)
    own_span = (units[:, None] // factor == np.arange(span)[None, :]).astype(np.float32)
    spread = (own_span @ sylvester(span)).astype(ml_dtypes.bfloat16)
    spread_t = np.ascontiguousarray(own_span.T).astype(ml_dtypes.bfloat16)
    pick_t = np.ascontiguousarray(pick.T)
    vmem = pl.BlockSpec(memory_space=pltpu.VMEM)
    anywhere = pl.BlockSpec(memory_space=pl.ANY)
    dma = pltpu.SemaphoreType.DMA
    small = (n_ten, tokens // groups, width)
    halves = (2, groups, tokens // groups, width)
    return pl.pallas_call(
        kernel,
        out_shape=jax.ShapeDtypeStruct((tokens, columns), BF16),
        in_specs=[anywhere, anywhere, anywhere, vmem, vmem, anywhere, vmem, vmem, vmem] + [vmem] * 4,
        out_specs=vmem,
        scratch_shapes=[
            pltpu.VMEM((tokens, features), BF16),
            pltpu.VMEM((2, n_seq, tokens // 2, depth), BF16),
            pltpu.VMEM((4, depth, width), BF16),
            pltpu.VMEM((2, width, columns), BF16),
            pltpu.VMEM((width, width), BF16),
            pltpu.VMEM((4, 2, 4, SIDE, tokens // 2, width), BF16),
            pltpu.VMEM((3, 2, 4, tokens // 2, width), BF16),
            pltpu.VMEM((2, 4, tokens // 2, width), F32),
            pltpu.VMEM((tokens, 128), F32),
            pltpu.VMEM(halves, BF16),
            pltpu.VMEM(small, BF16),
            pltpu.VMEM(small, BF16),
            pltpu.VMEM(halves, BF16),
            pltpu.VMEM((n_seq, 2, tokens, width), BF16),
            pltpu.VMEM((n_seq, tokens, columns), BF16),
            pltpu.VMEM((n_ten, tokens, columns), BF16),
            dma((7,)),
            dma((n_seq,)),
            dma((n_seq,)),
            dma((2,)),
            dma((3, 2, 4)),
            dma((3, 2, 4)),
            dma((3, 2, 4)),
            dma((3, 2, 4)),
            dma((n_ten,)),
            dma((n_ten,)),
            dma((n_ten,)),
            dma((n_ten,)),
            dma((30,)),
            dma((n_seq, 2)),
            dma((n_seq,)),
            dma((n_ten,)),
        ],
        compiler_params=pltpu.CompilerParams(
            collective_id=0, has_side_effects=True, vmem_limit_bytes=62 * 2**20
        ),
        cost_estimate=pl.CostEstimate(flops=11 * 10**9, bytes_accessed=12 * 10**6, transcendentals=10**6),
    )(
        hidden_in,
        gate_codes,
        up_codes,
        gate_scale.reshape(1, block),
        up_scale.reshape(1, block),
        down_codes,
        down_scale.reshape(1, columns),
        sign_bits.reshape(1, block),
        had52,
        pick,
        pick_t,
        spread,
        spread_t,
    )


def solution(mesh):
    return jax.shard_map(
        per_device,
        mesh=mesh,
        in_specs=(
            P("seq", None),
            P("seq", "tensor"),
            P("seq", "tensor"),
            P("tensor"),
            P("tensor"),
            P("tensor", "seq"),
            P("seq"),
            P("tensor"),
            P(),
        ),
        out_specs=P("tensor", "seq"),
        check_vma=False,
    )
```

```python
import functools
import math

import jax
import jax.numpy as jnp
import ml_dtypes
import numpy as np
from jax import lax
from jax.experimental import pallas as pl
from jax.experimental.pallas import tpu as pltpu
from jax.sharding import PartitionSpec as P

FF = 53248
SIDE = 4
MESH = pl.DeviceIdType.MESH
F32 = jnp.float32
BF16 = jnp.bfloat16


def mod(value, by):
    return lax.rem(value, by)


def kernel(
    hid_hbm, gate_hbm, up_hbm, gate_scale_hbm, up_scale_hbm, down_hbm, down_scale_hbm, signs_hbm, had_hbm,
    pick_hbm, pick_t_hbm, spread_hbm, spread_t_hbm,
    out_ref,
    gate_scale, up_scale, down_scale, signs, had, pick, pick_t, spread, spread_t, hid, x, w, wd, wx, ring, ring2, fin, inv, z1s, z1r, z2s, z2r, ag, acc, outs, outr,
    load_sem, xs, xr, core_sem, r1s, r1r, r2s, r2r, z1ss, z1rs, z2ss, z2rs, ags, agr, os, orr,
):
    seq = lax.axis_index("seq")
    ten = lax.axis_index("tensor")
    n_seq = SIDE * SIDE
    tokens, features = hid.shape
    depth = features // n_seq
    half_rows = tokens // 2
    n_ten = outr.shape[0]
    groups = n_ten // 2
    in_group = tokens // groups
    per_stream = groups // 2
    width = ring.shape[-1]
    core = mod(ten, 2)
    zed = lax.div(ten, 2)
    other = zed * 2 + 1 - core
    step_a = 1 + (SIDE - 1) * core
    step_b = SIDE - (SIDE - 1) * core
    pos_x, pos_y = mod(seq, SIDE), lax.div(seq, SIDE)
    pa = pos_x * (1 - core) + pos_y * core
    pb = pos_y * (1 - core) + pos_x * core

    def at(a, b):
        return mod(a + 2 * SIDE, SIDE) * step_a + mod(b + 2 * SIDE, SIDE) * step_b

    def remote(src, dst, send, recv, device):
        return pltpu.make_async_remote_copy(
            src_ref=src, dst_ref=dst, send_sem=send, recv_sem=recv, device_id=device, device_id_type=MESH
        )

    barrier = pltpu.get_barrier_semaphore()

    def greet_seq(d, c):
        pl.semaphore_signal(barrier, inc=1, device_id={"seq": mod(seq + d, n_seq)}, device_id_type=MESH)
        return c

    def greet_ten(d, c):
        pl.semaphore_signal(barrier, inc=1, device_id={"tensor": mod(ten + d, n_ten)}, device_id_type=MESH)
        return c

    lax.fori_loop(1, n_seq, greet_seq, 0)
    lax.fori_loop(1, n_ten, greet_ten, 0)

    loads = [pltpu.make_async_copy(hid_hbm, hid, load_sem.at[0])]
    for j, (source, part) in enumerate(((gate_hbm, 0), (up_hbm, 0), (gate_hbm, 1), (up_hbm, 1))):
        loads.append(
            pltpu.make_async_copy(source.at[:, part * width : (part + 1) * width], w.at[j], load_sem.at[1 + j])
        )
    for h in range(2):
        loads.append(
            pltpu.make_async_copy(down_hbm.at[h * width : (h + 1) * width, :], wd.at[h], load_sem.at[5 + h])
        )
    small = (
        (gate_scale_hbm, gate_scale), (up_scale_hbm, up_scale), (down_scale_hbm, down_scale), (signs_hbm, signs),
        (had_hbm, had), (pick_hbm, pick), (pick_t_hbm, pick_t), (spread_hbm, spread), (spread_t_hbm, spread_t),
    )
    for i, (source, target) in enumerate(small):
        loads.append(pltpu.make_async_copy(source, target, load_sem.at[7 + i]))
    for load in loads:
        load.start()
    pl.semaphore_wait(barrier, n_seq + n_ten - 2)

    my_rows = pl.ds(pl.multiple_of(core * half_rows, half_rows), half_rows)

    def piece(d):
        peer = mod(seq + d, n_seq)
        return remote(
            hid_hbm.at[my_rows, pl.ds(pl.multiple_of(peer * depth, depth), depth)],
            x.at[core, seq],
            xs.at[d],
            xr.at[d],
            {"seq": peer},
        )

    def send_piece(d, c):
        piece(d).start()
        return c

    lax.fori_loop(1, n_seq, send_piece, 0)
    own = pltpu.make_async_copy(
        hid_hbm.at[my_rows, pl.ds(pl.multiple_of(seq * depth, depth), depth)], x.at[core, seq], xs.at[0]
    )
    own.start()

    loads[0].wait()
    chunk = min(1024, features)

    def squares(i, total):
        part = hid[:, pl.ds(pl.multiple_of(i * chunk, chunk), chunk)].astype(F32)
        return total + jnp.sum(part * part, axis=1, keepdims=True)

    total = lax.fori_loop(0, features // chunk, squares, jnp.zeros((tokens, 1), F32))
    inv[...] = jnp.broadcast_to(lax.rsqrt(total * (1.0 / features) + 1e-05), inv.shape)

    own.wait()

    def got_piece(d, c):
        piece(d).wait_recv()
        return c

    lax.fori_loop(1, n_seq, got_piece, 0)
    swap = remote(x.at[core], x.at[core], core_sem.at[0], core_sem.at[1], {"tensor": other})
    swap.start()
    lend = []
    for h in range(2):
        lend.append(
            remote(
                down_hbm.at[h * width : (h + 1) * width, :],
                wx.at[h],
                core_sem.at[2 + 2 * h],
                core_sem.at[3 + 2 * h],
                {"tensor": other},
            )
        )
        lend[h].start()
    for load in loads[1:]:
        load.wait()
    swap.wait()

    def block_of(stream, step):
        return 3 - step if stream == 0 else 1 + step

    ahead = (1, SIDE - 1)

    def product(stream, step, j):
        a = pa + block_of(stream, step)
        rows = jnp.concatenate([x[stream, at(a, b)] for b in range(SIDE)], axis=0)
        return jnp.dot(rows, w[j], preferred_element_type=F32).reshape(SIDE, half_rows, width)

    def ring_copy(stream, step, j):
        return remote(
            ring.at[step, stream, j],
            ring.at[step + 1, stream, j],
            r1s.at[step, stream, j],
            r1r.at[step, stream, j],
            {"seq": at(pa + ahead[stream], pb)},
        )

    def ring2_copy(stream, step, j):
        if step == 0:
            source = ring.at[3, stream, j, mod(pb + block_of(stream, 0), SIDE)]
        else:
            source = ring2.at[step - 1, stream, j]
        return remote(
            source,
            ring2.at[step, stream, j],
            r2s.at[step, stream, j],
            r2r.at[step, stream, j],
            {"seq": at(pa, pb + ahead[stream])},
        )

    def first_axis(h, step):
        def go(j, c):
            for stream in range(2):
                value = product(stream, step, j)
                if step > 0:
                    ring_copy(stream, step - 1, j).wait_recv()
                    value = value + ring[step, stream, j].astype(F32)
                ring[step, stream, j] = value.astype(BF16)
                if step < 3:
                    ring_copy(stream, step, j).start()
                else:
                    ring2_copy(stream, 0, j).start()
            return c

        lax.fori_loop(2 * h, 2 * h + 2, go, 0)

    def second_axis(h, step):
        def go(j, c):
            for stream in range(2):
                ring2_copy(stream, step - 1, j).wait_recv()
                block = mod(pb + block_of(stream, step), SIDE)
                value = ring[3, stream, j, block].astype(F32) + ring2[step - 1, stream, j].astype(F32)
                if step < 3:
                    ring2[step - 1, stream, j] = value.astype(BF16)
                    ring2_copy(stream, step, j).start()
                else:
                    fin[stream, j] = value
            return c

        lax.fori_loop(2 * h, 2 * h + 2, go, 0)

    rows_at_once = 128

    def rows_of(r):
        return pl.ds(pl.multiple_of(r * rows_at_once, rows_at_once), rows_at_once)

    def combine():
        for copy in lend:
            copy.wait()
        sign = (1 - 2 * core).astype(F32)

        def go(r, c):
            rows = rows_of(r)
            d0, d1 = wd[0, rows, :].astype(F32), wd[1, rows, :].astype(F32)
            x0, x1 = wx[0, rows, :].astype(F32), wx[1, rows, :].astype(F32)
            wd[0, rows, :] = (x0 + x1 + sign * (d0 + d1)).astype(BF16)
            wd[1, rows, :] = (x0 - x1 + sign * (d0 - d1)).astype(BF16)
            return c

        lax.fori_loop(0, width // rows_at_once, go, 0)

    def rotate(first, last):
        def go(r, c):
            rows = rows_of(r)
            mixed = lax.dot_general(
                pick[rows, :], had[...].astype(F32).astype(BF16), (((1,), (1,)), ((), ())), preferred_element_type=F32
            )
            small = jnp.dot(mixed.astype(BF16), pick_t[...], preferred_element_type=F32)
            large = jnp.dot(spread[rows, :], spread_t[...], preferred_element_type=F32)
            matrix = (small * large).astype(BF16)
            for h in range(2):
                wx[h, rows, :] = jnp.dot(matrix, wd[h], preferred_element_type=F32).astype(BF16)
            return c

        count = width // rows_at_once
        lax.fori_loop(min(first, count), min(last, count), go, 0)

    def out_copy(h):
        def copy(d):
            peer = mod(zed + d, groups)
            return remote(
                z1s.at[h, peer], z1r.at[h, zed], z1ss.at[h, d], z1rs.at[h, d], {"tensor": peer * 2 + core}
            )

        return copy

    def back_copy(h):
        def copy(d):
            peer = mod(zed + d, groups)
            return remote(
                z2s.at[h, peer], z2r.at[h, zed], z2ss.at[h, d], z2rs.at[h, d], {"tensor": peer * 2 + core}
            )

        return copy

    def start_all(copy):
        def go(d, c):
            copy(d).start()
            return c

        lax.fori_loop(1, groups, go, 0)

    def arrive_all(copy):
        def go(d, c):
            copy(d).wait_recv()
            return c

        lax.fori_loop(1, groups, go, 0)

    def leave_all(copy):
        def go(d, c):
            copy(d).wait_send()
            return c

        lax.fori_loop(1, groups, go, 0)

    def activate(h):
        cols = slice(h * width, (h + 1) * width)
        for stream in range(2):
            rows = slice(stream * half_rows, (stream + 1) * half_rows)
            scale = inv[rows, 0:1]
            gate = fin[stream, 2 * h] * scale * gate_scale[cols].reshape(1, width)
            up = fin[stream, 2 * h + 1] * scale * up_scale[cols].reshape(1, width)
            act = gate / (1.0 + jnp.exp(-gate)) * up
            flipped = act * (1 - 2 * signs[cols].reshape(1, width)).astype(F32)
            z1s[h, stream * per_stream : (stream + 1) * per_stream] = flipped.reshape(
                per_stream, in_group, width
            ).astype(BF16)
        start_all(out_copy(h))
        z1r[h, zed] = z1s[h, zed]

    def mix(h):
        arrive_all(out_copy(h))
        value = z1r[h].astype(F32) * (1.0 / math.sqrt(FF))
        span = 1
        while span < groups:
            pairs = value.reshape(groups // (2 * span), 2, span * in_group, width)
            low, high = pairs[:, 0:1], pairs[:, 1:2]
            value = jnp.concatenate([low + high, low - high], axis=1)
            span *= 2
        z2s[h] = value.reshape(groups, in_group, width).astype(BF16)
        start_all(back_copy(h))
        z2r[h, zed] = z2s[h, zed]

    counts = [iter(range(30)), iter(range(30))]
    pending = []

    def pass_on(h, s, r, target):
        n = next(counts[h])
        copy = remote(ag.at[h, s, r], ag.at[h, s, r], ags.at[h, n], agr.at[h, s, r], {"seq": target})
        copy.start()
        pending.append(copy)

    def arrived(h, s, r):
        remote(ag.at[h, s, r], ag.at[h, s, r], ags.at[h, 0], agr.at[h, s, r], {"seq": seq}).wait_recv()

    def send_first(h, s, a_step, b_step):
        for r0, r1 in ((0, 1), (1, 0)):
            pass_on(h, s, r0, at(pa + a_step, pb + b_step))
            pass_on(h, s, r1, at(pa - a_step, pb - b_step))

    def gather_start(h):
        arrive_all(back_copy(h))
        ag[h, seq] = z2r[h].astype(F32).reshape(2, half_rows, width).astype(BF16)
        send_first(h, seq, 1, 0)
        send_first(h, seq, 0, 1)

    def gather_second(h):
        below, above = at(pa, pb - 1), at(pa, pb + 1)
        arrived(h, below, 0)
        pass_on(h, below, 0, above)
        arrived(h, above, 1)
        pass_on(h, above, 1, below)
        arrived(h, below, 1)
        send_first(h, below, 1, 0)
        arrived(h, above, 0)
        send_first(h, above, 1, 0)

    def gather_opposite(h):
        for r in range(2):
            arrived(h, at(pa, pb + 2), r)
        send_first(h, at(pa, pb + 2), 1, 0)

    def forward(h, b):
        arrived(h, at(pa - 1, b), 0)
        pass_on(h, at(pa - 1, b), 0, at(pa + 1, pb))
        arrived(h, at(pa + 1, b), 1)
        pass_on(h, at(pa + 1, b), 1, at(pa - 1, pb))

    def partial(s):
        return remote(outs.at[s], outr.at[ten], os.at[s], orr.at[ten], {"tensor": s})

    def multiply(h, blocks):
        rows = jnp.concatenate([ag[h, s].reshape(tokens, width) for s in blocks], axis=0)
        total = jnp.dot(rows, wx[h], preferred_element_type=F32)
        for i, s in enumerate(blocks):
            value = total[i * tokens : (i + 1) * tokens]
            if h == 0:
                acc[s] = value
                continue
            outs[s] = (value + acc[s]).astype(BF16)

            @pl.when(s != ten)
            def _():
                partial(s).start()

            @pl.when(s == ten)
            def _():
                outr[ten] = outs[s]

    def near(h, b):
        arrived(h, at(pa - 1, b), 1)
        arrived(h, at(pa + 1, b), 0)
        multiply(h, [at(pa, b), at(pa - 1, b), at(pa + 1, b)])

    def far(h, b):
        arrived(h, at(pa + 2, b), 0)
        arrived(h, at(pa + 2, b), 1)
        multiply(h, [at(pa + 2, b)])

    first_axis(0, 0)
    first_axis(0, 1)
    combine()
    first_axis(0, 2)
    rotate(0, 2)
    first_axis(1, 0)
    rotate(2, 4)
    first_axis(0, 3)
    rotate(4, 6)
    first_axis(1, 1)
    second_axis(0, 1)
    rotate(6, 8)
    second_axis(0, 2)
    first_axis(1, 2)
    second_axis(0, 3)
    activate(0)
    rotate(8, 11)
    first_axis(1, 3)
    mix(0)
    second_axis(1, 1)
    rotate(11, 13)
    second_axis(1, 2)
    gather_start(0)
    second_axis(1, 3)
    activate(1)
    gather_second(0)
    forward(0, pb)
    mix(1)
    gather_opposite(0)
    forward(0, pb - 1)
    forward(0, pb + 1)
    near(0, pb)
    far(0, pb)
    gather_start(1)
    forward(0, pb + 2)
    near(0, pb - 1)
    gather_second(1)
    far(0, pb - 1)
    forward(1, pb)
    near(0, pb + 1)
    gather_opposite(1)
    far(0, pb + 1)
    forward(1, pb - 1)
    near(0, pb + 2)
    far(0, pb + 2)
    near(1, pb)
    forward(1, pb + 1)
    far(1, pb)
    near(1, pb - 1)
    forward(1, pb + 2)
    far(1, pb - 1)
    near(1, pb + 1)
    far(1, pb + 1)
    near(1, pb + 2)
    far(1, pb + 2)

    def from_tensor(t, c):
        @pl.when(t != ten)
        def _():
            remote(outs.at[t], outr.at[t], os.at[t], orr.at[t], {"tensor": t}).wait()

        return c

    lax.fori_loop(0, n_ten, from_tensor, 0)
    total = outr[0].astype(F32)
    for t in range(1, n_ten):
        total = total + outr[t].astype(F32)
    out_ref[...] = (total * down_scale[...].reshape(1, -1)).astype(out_ref.dtype)

    def piece_left(d, c):
        piece(d).wait_send()
        return c

    lax.fori_loop(1, n_seq, piece_left, 0)

    def rings_left(j, c):
        for step in range(3):
            for stream in range(2):
                ring_copy(stream, step, j).wait_send()
                ring2_copy(stream, step, j).wait_send()
        return c

    lax.fori_loop(0, 4, rings_left, 0)
    for h in range(2):
        leave_all(out_copy(h))
        leave_all(back_copy(h))
    for copy in pending:
        copy.wait_send()


def sylvester(length):
    matrix = np.ones((1, 1), np.float32)
    while matrix.shape[0] < length:
        matrix = np.kron(np.array([[1, 1], [1, -1]], np.float32), matrix)
    return matrix


def per_device(
    hidden_in, gate_codes, up_codes, gate_scale, up_scale, down_codes, down_scale, sign_bits, had52
):
    tokens, features = hidden_in.shape
    depth, block = gate_codes.shape
    width = block // 2
    factor = had52.shape[0]
    span = width // factor
    columns = down_codes.shape[1]
    n_seq = SIDE * SIDE
    n_ten = lax.axis_size("tensor")
    groups = n_ten // 2
    units = np.arange(width)
    pick = (units[:, None] % factor == np.arange(factor)[None, :]).astype(ml_dtypes.bfloat16)
    own_span = (units[:, None] // factor == np.arange(span)[None, :]).astype(np.float32)
    spread = (own_span @ sylvester(span)).astype(ml_dtypes.bfloat16)
    spread_t = np.ascontiguousarray(own_span.T).astype(ml_dtypes.bfloat16)
    pick_t = np.ascontiguousarray(pick.T)
    vmem = pl.BlockSpec(memory_space=pltpu.VMEM)
    anywhere = pl.BlockSpec(memory_space=pl.ANY)
    dma = pltpu.SemaphoreType.DMA
    small = (2, groups, tokens // groups, width)
    return pl.pallas_call(
        kernel,
        out_shape=jax.ShapeDtypeStruct((tokens, columns), BF16),
        in_specs=[anywhere] * 13,
        out_specs=vmem,
        scratch_shapes=[
            pltpu.VMEM((block,), F32),
            pltpu.VMEM((block,), F32),
            pltpu.VMEM((columns,), F32),
            pltpu.VMEM((block,), jnp.int32),
            pltpu.VMEM((factor, factor), jnp.int32),
            pltpu.VMEM((width, factor), BF16),
            pltpu.VMEM((factor, width), BF16),
            pltpu.VMEM((width, span), BF16),
            pltpu.VMEM((span, width), BF16),
            pltpu.VMEM((tokens, features), BF16),
            pltpu.VMEM((2, n_seq, tokens // 2, depth), BF16),
            pltpu.VMEM((4, depth, width), BF16),
            pltpu.VMEM((2, width, columns), BF16),
            pltpu.VMEM((2, width, columns), BF16),
            pltpu.VMEM((4, 2, 4, SIDE, tokens // 2, width), BF16),
            pltpu.VMEM((3, 2, 4, tokens // 2, width), BF16),
            pltpu.VMEM((2, 4, tokens // 2, width), F32),
            pltpu.VMEM((tokens, 128), F32),
            pltpu.VMEM(small, BF16),
            pltpu.VMEM(small, BF16),
            pltpu.VMEM(small, BF16),
            pltpu.VMEM(small, BF16),
            pltpu.VMEM((2, n_seq, 2, tokens // 2, width), BF16),
            pltpu.VMEM((n_seq, tokens, columns), F32),
            pltpu.VMEM((n_seq, tokens, columns), BF16),
            pltpu.VMEM((n_ten, tokens, columns), BF16),
            dma((16,)),
            dma((n_seq,)),
            dma((n_seq,)),
            dma((6,)),
            dma((3, 2, 4)),
            dma((3, 2, 4)),
            dma((3, 2, 4)),
            dma((3, 2, 4)),
            dma((2, groups)),
            dma((2, groups)),
            dma((2, groups)),
            dma((2, groups)),
            dma((2, 30)),
            dma((2, n_seq, 2)),
            dma((n_seq,)),
            dma((n_ten,)),
        ],
        compiler_params=pltpu.CompilerParams(
            collective_id=0, has_side_effects=True, vmem_limit_bytes=62 * 2**20
        ),
        cost_estimate=pl.CostEstimate(flops=11 * 10**9, bytes_accessed=12 * 10**6, transcendentals=10**6),
    )(
        hidden_in,
        gate_codes,
        up_codes,
        gate_scale,
        up_scale,
        down_codes,
        down_scale,
        sign_bits,
        had52,
        pick,
        pick_t,
        spread,
        spread_t,
    )


def solution(mesh):
    return jax.shard_map(
        per_device,
        mesh=mesh,
        in_specs=(
            P("seq", None),
            P("seq", "tensor"),
            P("seq", "tensor"),
            P("tensor"),
            P("tensor"),
            P("tensor", "seq"),
            P("seq"),
            P("tensor"),
            P(),
        ),
        out_specs=P("tensor", "seq"),
        check_vma=False,
    )
```

```python
import functools
import math

import jax
import jax.numpy as jnp
import ml_dtypes
import numpy as np
from jax import lax
from jax.experimental import pallas as pl
from jax.experimental.pallas import tpu as pltpu
from jax.sharding import PartitionSpec as P

FF = 53248
SIDE = 4
MESH = pl.DeviceIdType.MESH
F32 = jnp.float32
BF16 = jnp.bfloat16


def mod(value, by):
    return lax.rem(value, by)


def kernel(
    hid_hbm, gate_hbm, up_hbm, gate_scale_hbm, up_scale_hbm, down_hbm, down_scale_hbm, signs_hbm, had_hbm,
    pick_hbm, pick_t_hbm, spread_hbm, spread_t_hbm,
    out_ref,
    gate_scale, up_scale, down_scale, signs, had, pick, pick_t, spread, spread_t, hid, x, w, wd, wx, ring, ring2, fin, inv, z1s, z1r, z2s, z2r, ag, acc, outs, outr,
    load_sem, xs, xr, core_sem, r1s, r1r, r2s, r2r, z1ss, z1rs, z2ss, z2rs, ags, agr, os, orr,
):
    seq = lax.axis_index("seq")
    ten = lax.axis_index("tensor")
    n_seq = SIDE * SIDE
    tokens, features = hid.shape
    depth = features // n_seq
    half_rows = tokens // 2
    n_ten = outr.shape[0]
    groups = n_ten // 2
    in_group = tokens // groups
    per_stream = groups // 2
    width = ring.shape[-1]
    core = mod(ten, 2)
    zed = lax.div(ten, 2)
    other = zed * 2 + 1 - core
    step_a = 1 + (SIDE - 1) * core
    step_b = SIDE - (SIDE - 1) * core
    pos_x, pos_y = mod(seq, SIDE), lax.div(seq, SIDE)
    pa = pos_x * (1 - core) + pos_y * core
    pb = pos_y * (1 - core) + pos_x * core

    def at(a, b):
        return mod(a + 2 * SIDE, SIDE) * step_a + mod(b + 2 * SIDE, SIDE) * step_b

    def remote(src, dst, send, recv, device):
        return pltpu.make_async_remote_copy(
            src_ref=src, dst_ref=dst, send_sem=send, recv_sem=recv, device_id=device, device_id_type=MESH
        )

    barrier = pltpu.get_barrier_semaphore()

    def greet_seq(d, c):
        pl.semaphore_signal(barrier, inc=1, device_id={"seq": mod(seq + d, n_seq)}, device_id_type=MESH)
        return c

    def greet_ten(d, c):
        pl.semaphore_signal(barrier, inc=1, device_id={"tensor": mod(ten + d, n_ten)}, device_id_type=MESH)
        return c

    lax.fori_loop(1, n_seq, greet_seq, 0)
    lax.fori_loop(1, n_ten, greet_ten, 0)

    loads = [pltpu.make_async_copy(hid_hbm, hid, load_sem.at[0])]
    for j, (source, part) in enumerate(((gate_hbm, 0), (up_hbm, 0), (gate_hbm, 1), (up_hbm, 1))):
        loads.append(
            pltpu.make_async_copy(source.at[:, part * width : (part + 1) * width], w.at[j], load_sem.at[1 + j])
        )
    for h in range(2):
        loads.append(
            pltpu.make_async_copy(down_hbm.at[h * width : (h + 1) * width, :], wd.at[h], load_sem.at[5 + h])
        )
    small = (
        (gate_scale_hbm, gate_scale), (up_scale_hbm, up_scale), (down_scale_hbm, down_scale), (signs_hbm, signs),
        (had_hbm, had), (pick_hbm, pick), (pick_t_hbm, pick_t), (spread_hbm, spread), (spread_t_hbm, spread_t),
    )
    for i, (source, target) in enumerate(small):
        loads.append(pltpu.make_async_copy(source, target, load_sem.at[7 + i]))
    pl.semaphore_wait(barrier, n_seq + n_ten - 2)

    my_rows = pl.ds(pl.multiple_of(core * half_rows, half_rows), half_rows)

    def piece(d):
        peer = mod(seq + d, n_seq)
        return remote(
            hid_hbm.at[my_rows, pl.ds(pl.multiple_of(peer * depth, depth), depth)],
            x.at[core, seq],
            xs.at[d],
            xr.at[d],
            {"seq": peer},
        )

    def send_piece(d, c):
        piece(d).start()
        return c

    lax.fori_loop(1, n_seq, send_piece, 0)
    own = pltpu.make_async_copy(
        hid_hbm.at[my_rows, pl.ds(pl.multiple_of(seq * depth, depth), depth)], x.at[core, seq], xs.at[0]
    )
    own.start()
    for load in loads:
        load.start()

    loads[0].wait()
    chunk = min(1024, features)

    def squares(i, total):
        part = hid[:, pl.ds(pl.multiple_of(i * chunk, chunk), chunk)].astype(F32)
        return total + jnp.sum(part * part, axis=1, keepdims=True)

    total = lax.fori_loop(0, features // chunk, squares, jnp.zeros((tokens, 1), F32))
    inv[...] = jnp.broadcast_to(lax.rsqrt(total * (1.0 / features) + 1e-05), inv.shape)

    own.wait()

    def got_piece(d, c):
        piece(d).wait_recv()
        return c

    lax.fori_loop(1, n_seq, got_piece, 0)
    swap = remote(x.at[core], x.at[core], core_sem.at[0], core_sem.at[1], {"tensor": other})
    swap.start()
    lend = []
    for h in range(2):
        lend.append(
            remote(
                down_hbm.at[h * width : (h + 1) * width, :],
                wx.at[h],
                core_sem.at[2 + 2 * h],
                core_sem.at[3 + 2 * h],
                {"tensor": other},
            )
        )
        lend[h].start()
    for load in loads[1:]:
        load.wait()
    swap.wait()

    def block_of(stream, step):
        return 3 - step if stream == 0 else 1 + step

    ahead = (1, SIDE - 1)

    def product(stream, step, j):
        a = pa + block_of(stream, step)
        rows = jnp.concatenate([x[stream, at(a, b)] for b in range(SIDE)], axis=0)
        return jnp.dot(rows, w[j], preferred_element_type=F32).reshape(SIDE, half_rows, width)

    def ring_copy(stream, step, j):
        return remote(
            ring.at[step, stream, j],
            ring.at[step + 1, stream, j],
            r1s.at[step, stream, j],
            r1r.at[step, stream, j],
            {"seq": at(pa + ahead[stream], pb)},
        )

    def ring2_copy(stream, step, j):
        if step == 0:
            source = ring.at[3, stream, j, mod(pb + block_of(stream, 0), SIDE)]
        else:
            source = ring2.at[step - 1, stream, j]
        return remote(
            source,
            ring2.at[step, stream, j],
            r2s.at[step, stream, j],
            r2r.at[step, stream, j],
            {"seq": at(pa, pb + ahead[stream])},
        )

    def first_axis(h, step):
        def go(j, c):
            for stream in range(2):
                value = product(stream, step, j)
                if step > 0:
                    ring_copy(stream, step - 1, j).wait_recv()
                    value = value + ring[step, stream, j].astype(F32)
                ring[step, stream, j] = value.astype(BF16)
                if step < 3:
                    ring_copy(stream, step, j).start()
                else:
                    ring2_copy(stream, 0, j).start()
            return c

        lax.fori_loop(2 * h, 2 * h + 2, go, 0)

    def second_axis(h, step):
        def go(j, c):
            for stream in range(2):
                ring2_copy(stream, step - 1, j).wait_recv()
                block = mod(pb + block_of(stream, step), SIDE)
                value = ring[3, stream, j, block].astype(F32) + ring2[step - 1, stream, j].astype(F32)
                if step < 3:
                    ring2[step - 1, stream, j] = value.astype(BF16)
                    ring2_copy(stream, step, j).start()
                else:
                    fin[stream, j] = value
            return c

        lax.fori_loop(2 * h, 2 * h + 2, go, 0)

    rows_at_once = 128

    def rows_of(r):
        return pl.ds(pl.multiple_of(r * rows_at_once, rows_at_once), rows_at_once)

    def combine():
        for copy in lend:
            copy.wait()
        sign = (1 - 2 * core).astype(F32)

        def go(r, c):
            rows = rows_of(r)
            d0, d1 = wd[0, rows, :].astype(F32), wd[1, rows, :].astype(F32)
            x0, x1 = wx[0, rows, :].astype(F32), wx[1, rows, :].astype(F32)
            wd[0, rows, :] = (x0 + x1 + sign * (d0 + d1)).astype(BF16)
            wd[1, rows, :] = (x0 - x1 + sign * (d0 - d1)).astype(BF16)
            return c

        lax.fori_loop(0, width // rows_at_once, go, 0)

    def rotate(first, last):
        def go(r, c):
            rows = rows_of(r)
            mixed = lax.dot_general(
                pick[rows, :], had[...].astype(F32).astype(BF16), (((1,), (1,)), ((), ())), preferred_element_type=F32
            )
            small = jnp.dot(mixed.astype(BF16), pick_t[...], preferred_element_type=F32)
            large = jnp.dot(spread[rows, :], spread_t[...], preferred_element_type=F32)
            matrix = (small * large).astype(BF16)
            for h in range(2):
                wx[h, rows, :] = jnp.dot(matrix, wd[h], preferred_element_type=F32).astype(BF16)
            return c

        count = width // rows_at_once
        lax.fori_loop(min(first, count), min(last, count), go, 0)

    def out_copy(h):
        def copy(d):
            peer = mod(zed + d, groups)
            return remote(
                z1s.at[h, peer], z1r.at[h, zed], z1ss.at[h, d], z1rs.at[h, d], {"tensor": peer * 2 + core}
            )

        return copy

    def back_copy(h):
        def copy(d):
            peer = mod(zed + d, groups)
            return remote(
                z2s.at[h, peer], z2r.at[h, zed], z2ss.at[h, d], z2rs.at[h, d], {"tensor": peer * 2 + core}
            )

        return copy

    def start_all(copy):
        def go(d, c):
            copy(d).start()
            return c

        lax.fori_loop(1, groups, go, 0)

    def arrive_all(copy):
        def go(d, c):
            copy(d).wait_recv()
            return c

        lax.fori_loop(1, groups, go, 0)

    def leave_all(copy):
        def go(d, c):
            copy(d).wait_send()
            return c

        lax.fori_loop(1, groups, go, 0)

    def activate(h):
        cols = slice(h * width, (h + 1) * width)
        for stream in range(2):
            rows = slice(stream * half_rows, (stream + 1) * half_rows)
            scale = inv[rows, 0:1]
            gate = fin[stream, 2 * h] * scale * gate_scale[cols].reshape(1, width)
            up = fin[stream, 2 * h + 1] * scale * up_scale[cols].reshape(1, width)
            act = gate / (1.0 + jnp.exp(-gate)) * up
            flipped = act * (1 - 2 * signs[cols].reshape(1, width)).astype(F32)
            z1s[h, stream * per_stream : (stream + 1) * per_stream] = flipped.reshape(
                per_stream, in_group, width
            ).astype(BF16)
        start_all(out_copy(h))
        z1r[h, zed] = z1s[h, zed]

    def mix(h):
        arrive_all(out_copy(h))
        value = z1r[h].astype(F32) * (1.0 / math.sqrt(FF))
        span = 1
        while span < groups:
            pairs = value.reshape(groups // (2 * span), 2, span * in_group, width)
            low, high = pairs[:, 0:1], pairs[:, 1:2]
            value = jnp.concatenate([low + high, low - high], axis=1)
            span *= 2
        z2s[h] = value.reshape(groups, in_group, width).astype(BF16)
        start_all(back_copy(h))
        z2r[h, zed] = z2s[h, zed]

    counts = [iter(range(30)), iter(range(30))]
    pending = []

    def pass_on(h, s, r, target):
        n = next(counts[h])
        copy = remote(ag.at[h, s, r], ag.at[h, s, r], ags.at[h, n], agr.at[h, s, r], {"seq": target})
        copy.start()
        pending.append(copy)

    def arrived(h, s, r):
        remote(ag.at[h, s, r], ag.at[h, s, r], ags.at[h, 0], agr.at[h, s, r], {"seq": seq}).wait_recv()

    def send_first(h, s, a_step, b_step):
        for r0, r1 in ((0, 1), (1, 0)):
            pass_on(h, s, r0, at(pa + a_step, pb + b_step))
            pass_on(h, s, r1, at(pa - a_step, pb - b_step))

    def gather_start(h):
        arrive_all(back_copy(h))
        ag[h, seq] = z2r[h].astype(F32).reshape(2, half_rows, width).astype(BF16)
        send_first(h, seq, 1, 0)
        send_first(h, seq, 0, 1)

    def gather_second(h):
        below, above = at(pa, pb - 1), at(pa, pb + 1)
        arrived(h, below, 0)
        pass_on(h, below, 0, above)
        arrived(h, above, 1)
        pass_on(h, above, 1, below)
        arrived(h, below, 1)
        send_first(h, below, 1, 0)
        arrived(h, above, 0)
        send_first(h, above, 1, 0)

    def gather_opposite(h):
        for r in range(2):
            arrived(h, at(pa, pb + 2), r)
        send_first(h, at(pa, pb + 2), 1, 0)

    def forward(h, b):
        arrived(h, at(pa - 1, b), 0)
        pass_on(h, at(pa - 1, b), 0, at(pa + 1, pb))
        arrived(h, at(pa + 1, b), 1)
        pass_on(h, at(pa + 1, b), 1, at(pa - 1, pb))

    def partial(s):
        return remote(outs.at[s], outr.at[ten], os.at[s], orr.at[ten], {"tensor": s})

    def multiply(h, blocks):
        rows = jnp.concatenate([ag[h, s].reshape(tokens, width) for s in blocks], axis=0)
        total = jnp.dot(rows, wx[h], preferred_element_type=F32)
        for i, s in enumerate(blocks):
            value = total[i * tokens : (i + 1) * tokens]
            if h == 0:
                acc[s] = value
                continue
            outs[s] = (value + acc[s]).astype(BF16)

            @pl.when(s != ten)
            def _():
                partial(s).start()

            @pl.when(s == ten)
            def _():
                outr[ten] = outs[s]

    def near(h, b):
        arrived(h, at(pa - 1, b), 1)
        arrived(h, at(pa + 1, b), 0)
        multiply(h, [at(pa, b), at(pa - 1, b), at(pa + 1, b)])

    def far(h, b):
        arrived(h, at(pa + 2, b), 0)
        arrived(h, at(pa + 2, b), 1)
        multiply(h, [at(pa + 2, b)])

    first_axis(0, 0)
    first_axis(0, 1)
    combine()
    first_axis(0, 2)
    rotate(0, 2)
    first_axis(1, 0)
    rotate(2, 4)
    first_axis(0, 3)
    rotate(4, 6)
    first_axis(1, 1)
    second_axis(0, 1)
    rotate(6, 8)
    second_axis(0, 2)
    first_axis(1, 2)
    second_axis(0, 3)
    activate(0)
    rotate(8, 11)
    first_axis(1, 3)
    mix(0)
    second_axis(1, 1)
    rotate(11, 13)
    second_axis(1, 2)
    gather_start(0)
    second_axis(1, 3)
    activate(1)
    gather_second(0)
    forward(0, pb)
    mix(1)
    gather_opposite(0)
    forward(0, pb - 1)
    forward(0, pb + 1)
    near(0, pb)
    far(0, pb)
    gather_start(1)
    forward(0, pb + 2)
    near(0, pb - 1)
    gather_second(1)
    far(0, pb - 1)
    forward(1, pb)
    near(0, pb + 1)
    gather_opposite(1)
    far(0, pb + 1)
    forward(1, pb - 1)
    near(0, pb + 2)
    far(0, pb + 2)
    near(1, pb)
    forward(1, pb + 1)
    far(1, pb)
    near(1, pb - 1)
    forward(1, pb + 2)
    far(1, pb - 1)
    near(1, pb + 1)
    far(1, pb + 1)
    near(1, pb + 2)
    far(1, pb + 2)

    def from_tensor(t, c):
        @pl.when(t != ten)
        def _():
            remote(outs.at[t], outr.at[t], os.at[t], orr.at[t], {"tensor": t}).wait()

        return c

    lax.fori_loop(0, n_ten, from_tensor, 0)
    total = outr[0].astype(F32)
    for t in range(1, n_ten):
        total = total + outr[t].astype(F32)
    out_ref[...] = (total * down_scale[...].reshape(1, -1)).astype(out_ref.dtype)

    def piece_left(d, c):
        piece(d).wait_send()
        return c

    lax.fori_loop(1, n_seq, piece_left, 0)

    def rings_left(j, c):
        for step in range(3):
            for stream in range(2):
                ring_copy(stream, step, j).wait_send()
                ring2_copy(stream, step, j).wait_send()
        return c

    lax.fori_loop(0, 4, rings_left, 0)
    for h in range(2):
        leave_all(out_copy(h))
        leave_all(back_copy(h))
    for copy in pending:
        copy.wait_send()


def sylvester(length):
    matrix = np.ones((1, 1), np.float32)
    while matrix.shape[0] < length:
        matrix = np.kron(np.array([[1, 1], [1, -1]], np.float32), matrix)
    return matrix


def per_device(
    hidden_in, gate_codes, up_codes, gate_scale, up_scale, down_codes, down_scale, sign_bits, had52
):
    tokens, features = hidden_in.shape
    depth, block = gate_codes.shape
    width = block // 2
    factor = had52.shape[0]
    span = width // factor
    columns = down_codes.shape[1]
    n_seq = SIDE * SIDE
    n_ten = lax.axis_size("tensor")
    groups = n_ten // 2
    units = np.arange(width)
    pick = (units[:, None] % factor == np.arange(factor)[None, :]).astype(ml_dtypes.bfloat16)
    own_span = (units[:, None] // factor == np.arange(span)[None, :]).astype(np.float32)
    spread = (own_span @ sylvester(span)).astype(ml_dtypes.bfloat16)
    spread_t = np.ascontiguousarray(own_span.T).astype(ml_dtypes.bfloat16)
    pick_t = np.ascontiguousarray(pick.T)
    vmem = pl.BlockSpec(memory_space=pltpu.VMEM)
    anywhere = pl.BlockSpec(memory_space=pl.ANY)
    dma = pltpu.SemaphoreType.DMA
    small = (2, groups, tokens // groups, width)
    return pl.pallas_call(
        kernel,
        out_shape=jax.ShapeDtypeStruct((tokens, columns), BF16),
        in_specs=[anywhere] * 13,
        out_specs=vmem,
        scratch_shapes=[
            pltpu.VMEM((block,), F32),
            pltpu.VMEM((block,), F32),
            pltpu.VMEM((columns,), F32),
            pltpu.VMEM((block,), jnp.int32),
            pltpu.VMEM((factor, factor), jnp.int32),
            pltpu.VMEM((width, factor), BF16),
            pltpu.VMEM((factor, width), BF16),
            pltpu.VMEM((width, span), BF16),
            pltpu.VMEM((span, width), BF16),
            pltpu.VMEM((tokens, features), BF16),
            pltpu.VMEM((2, n_seq, tokens // 2, depth), BF16),
            pltpu.VMEM((4, depth, width), BF16),
            pltpu.VMEM((2, width, columns), BF16),
            pltpu.VMEM((2, width, columns), BF16),
            pltpu.VMEM((4, 2, 4, SIDE, tokens // 2, width), BF16),
            pltpu.VMEM((3, 2, 4, tokens // 2, width), BF16),
            pltpu.VMEM((2, 4, tokens // 2, width), F32),
            pltpu.VMEM((tokens, 128), F32),
            pltpu.VMEM(small, BF16),
            pltpu.VMEM(small, BF16),
            pltpu.VMEM(small, BF16),
            pltpu.VMEM(small, BF16),
            pltpu.VMEM((2, n_seq, 2, tokens // 2, width), BF16),
            pltpu.VMEM((n_seq, tokens, columns), F32),
            pltpu.VMEM((n_seq, tokens, columns), BF16),
            pltpu.VMEM((n_ten, tokens, columns), BF16),
            dma((16,)),
            dma((n_seq,)),
            dma((n_seq,)),
            dma((6,)),
            dma((3, 2, 4)),
            dma((3, 2, 4)),
            dma((3, 2, 4)),
            dma((3, 2, 4)),
            dma((2, groups)),
            dma((2, groups)),
            dma((2, groups)),
            dma((2, groups)),
            dma((2, 30)),
            dma((2, n_seq, 2)),
            dma((n_seq,)),
            dma((n_ten,)),
        ],
        compiler_params=pltpu.CompilerParams(
            collective_id=0, has_side_effects=True, vmem_limit_bytes=62 * 2**20
        ),
        cost_estimate=pl.CostEstimate(flops=11 * 10**9, bytes_accessed=12 * 10**6, transcendentals=10**6),
    )(
        hidden_in,
        gate_codes,
        up_codes,
        gate_scale,
        up_scale,
        down_codes,
        down_scale,
        sign_bits,
        had52,
        pick,
        pick_t,
        spread,
        spread_t,
    )


def solution(mesh):
    return jax.shard_map(
        per_device,
        mesh=mesh,
        in_specs=(
            P("seq", None),
            P("seq", "tensor"),
            P("seq", "tensor"),
            P("tensor"),
            P("tensor"),
            P("tensor", "seq"),
            P("seq"),
            P("tensor"),
            P(),
        ),
        out_specs=P("tensor", "seq"),
        check_vma=False,
    )
```
